256 devices in a mesh: dap: 64 (over x, z, y_hi), head: 4 (over y_lo, core).
Axes of the slice: x: 4, y: 4 (y_hi: 2, y_lo: 2; y = y_hi * 2 + y_lo), z: 8, core: 2. Of those that a mesh axis runs over, the one named last changes fastest.
Arguments:
- pair: bfloat16 [1024, 1024, 128], P('dap'), may hold values from -600 to 600
- residue_mask: int32 [1024], replicated, may hold values 0 or 1
- chain_breaks: int32 [1024], replicated, may hold values 0 or 1
- w_query: bfloat16 [128, 128], P(None, 'head'), may hold values from -0.5 to 0.5
- w_key: bfloat16 [128, 128], P(None, 'head'), may hold values from -0.5 to 0.5
- w_value: bfloat16 [128, 128], P(None, 'head'), may hold values from -0.5 to 0.5
- w_gate: bfloat16 [128, 128], P(None, 'head'), may hold values from -0.5 to 0.5
- w_bias: bfloat16 [128, 4], P(None, 'head'), may hold values from -29 to 29
- w_out: bfloat16 [128, 128], P('head'), may hold values from -0.5 to 0.5
Outputs:
- update: bfloat16 [1024, 1024, 128], P('dap', None, 'head')
The draws below stay inside these ranges and needn't reach their ends.
All inputs are finite; a program needn't handle non-finite values.
Results may differ from the reference program's by a relative error of at most 0.019.
Values may be sent and summed in bfloat16 or wider, within the bound.
No kernel may reach another device: no remote copies, remote signals or barrier semaphores. Data moves between devices by JAX's collectives and lax.ppermute only.
A program may use at most 64 MiB of HBM per device.

```python
import math
import jax
import jax.numpy as jnp
from jax import lax

PAIR = 128
HEADS = 4
HEAD_DIM = 32
RESIDUES = 1024


def draw_pair(key, part):
    key = jax.random.fold_in(key, 11)
    first, second, third = jax.random.split(key, 3)
    entry_scale = jnp.exp(jax.random.uniform(second, (RESIDUES, RESIDUES, 1), minval=0.0, maxval=math.log(10.0)))
    channel_scale = jnp.exp(jax.random.uniform(third, (1, 1, PAIR), minval=0.0, maxval=math.log(10.0)))
    base = jnp.clip(jax.random.normal(first, (RESIDUES, RESIDUES, PAIR)), -6.0, 6.0)
    return (base * entry_scale * channel_scale).astype(jnp.bfloat16)


def draw_w_bias(key, part):
    key = jax.random.fold_in(key, 5)
    first, second = jax.random.split(key)
    base = jnp.clip(jax.random.normal(first, (PAIR, HEADS)), -4.0, 4.0)
    strength = jnp.exp(jax.random.uniform(second, (1, HEADS), minval=0.0, maxval=math.log(3.0)))
    return (base * strength * 0.0884).astype(jnp.bfloat16)


def set_ends(values, stream_key, low, high):
    place = [jax.random.randint(jax.random.fold_in(stream_key, axis), (), 0, length) for axis, length in enumerate(values.shape)]
    main_axis = values.shape.index(max(values.shape))
    next_to = place[:main_axis] + [(place[main_axis] + 1) % values.shape[main_axis]] + place[main_axis + 1:]
    return values.at[tuple(place)].set(low).at[tuple(next_to)].set(high)


def steps_of(key, dims, cuts, smallest, high):
    loudness, own = 1.0, jax.random.fold_in(key, 6)
    for dim, parts in cuts:
        heights = jnp.exp(jax.random.uniform(jax.random.fold_in(own, dim), (parts,), jnp.float32, smallest / len(cuts), high / len(cuts)))
        loudness = loudness * jnp.repeat(heights, dims[dim] // parts).reshape([-1 if axis == dim else 1 for axis in range(len(dims))])
    return loudness


def centred(stream_key, dims, width, limit, cuts=(), held_as=jnp.bfloat16):
    level = steps_of(stream_key, dims, cuts, -0.22, 0.18) if cuts else 1.0
    drawn = jax.random.normal(stream_key, dims, jnp.float32) * width * level
    return jnp.minimum(jnp.maximum(drawn, -limit), limit).astype(held_as)


def setup_inputs(seed: int = 0) -> dict:
    seeds = jax.random.split(jax.random.key(seed), 10)
    return {
        "pair": draw_pair(jax.random.fold_in(seeds[9], 71), 0),
        "residue_mask": set_ends((jax.random.randint(seeds[1], (RESIDUES,), 0, 8) < 7).astype(jnp.int32), jax.random.fold_in(seeds[1], 1), 0, 1),
        "chain_breaks": set_ends((jax.random.randint(seeds[2], (RESIDUES,), 0, 32) < 1).astype(jnp.int32), jax.random.fold_in(seeds[2], 1), 0, 1),
        "w_query": centred(seeds[3], (PAIR, HEADS * HEAD_DIM), PAIR ** -0.5, 0.5, ((1, 4),)),
        "w_key": centred(seeds[4], (PAIR, HEADS * HEAD_DIM), PAIR ** -0.5, 0.5, ((1, 4),)),
        "w_value": centred(seeds[5], (PAIR, HEADS * HEAD_DIM), PAIR ** -0.5, 0.5, ((1, 4),)),
        "w_gate": centred(seeds[6], (PAIR, HEADS * HEAD_DIM), PAIR ** -0.5, 0.5, ((1, 4),)),
        "w_bias": draw_w_bias(jax.random.fold_in(seeds[9], 71), 0),
        "w_out": centred(seeds[8], (HEADS * HEAD_DIM, PAIR), (HEADS * HEAD_DIM) ** -0.5, 0.5, ((0, 4),)),
    }


chain_penalty = 2.0
masked_score = -1000000000.0

def normalize(pair):
    x = pair.astype(jnp.float32)
    mean = lax.optimization_barrier(jnp.mean(x, -1, keepdims=True))
    centered = x - mean
    variance = lax.optimization_barrier(jnp.mean(centered * centered, -1, keepdims=True))
    return (centered * lax.rsqrt(variance + 1e-05)).astype(jnp.bfloat16)

def reference(pair, residue_mask, chain_breaks, w_query, w_key, w_value, w_gate, w_bias, w_out):
    normed = normalize(pair)
    query = (jnp.dot(normed, w_query, preferred_element_type=jnp.float32) * HEAD_DIM ** (-0.5)).astype(jnp.bfloat16)
    keys = jnp.dot(normed, w_key, preferred_element_type=jnp.float32).astype(jnp.bfloat16)
    values = jnp.dot(normed, w_value, preferred_element_type=jnp.float32).astype(jnp.bfloat16)
    gate = jax.nn.sigmoid(jnp.dot(normed, w_gate, preferred_element_type=jnp.float32)).astype(jnp.bfloat16)
    bias = jnp.dot(normed, w_bias, preferred_element_type=jnp.float32).astype(jnp.bfloat16)
    bias = jnp.transpose(bias, (2, 0, 1)).astype(jnp.float32)
    chain = jnp.cumsum(chain_breaks).astype(jnp.int32)
    penalty = jnp.where(chain[:, None] == chain[None, :], 0.0, -chain_penalty).astype(jnp.float32)
    keep = residue_mask[:, None] > 0

    def column(index):
        q = lax.dynamic_index_in_dim(query, index, 1, keepdims=False).reshape(RESIDUES, HEADS, HEAD_DIM).astype(jnp.float32)
        k = lax.dynamic_index_in_dim(keys, index, 1, keepdims=False).reshape(RESIDUES, HEADS, HEAD_DIM).astype(jnp.float32)
        v = lax.dynamic_index_in_dim(values, index, 1, keepdims=False).reshape(RESIDUES, HEADS, HEAD_DIM).astype(jnp.float32)
        scores = jnp.einsum('khc,ihc->hki', k, q) + bias + penalty
        scores = jnp.where(keep, scores, masked_score)
        weights = jax.nn.softmax(scores, axis=1).astype(jnp.bfloat16).astype(jnp.float32)
        result = jnp.einsum('hki,khc->ihc', weights, v)
        return result.astype(jnp.bfloat16).reshape(RESIDUES, HEADS * HEAD_DIM)
    attended = lax.map(column, jnp.arange(RESIDUES, dtype=jnp.int32))
    attended = jnp.swapaxes(attended, 0, 1)
    gated = (gate.astype(jnp.float32) * attended.astype(jnp.float32)).astype(jnp.bfloat16)
    return jnp.dot(gated, w_out, preferred_element_type=jnp.float32).astype(jnp.bfloat16)
```

```python
import functools
import math

import jax
import jax.numpy as jnp
from jax import lax
from jax.experimental import pallas as pl
from jax.experimental.pallas import tpu as pltpu
from jax.sharding import PartitionSpec as P

bf16 = jnp.bfloat16
f32 = jnp.float32

N = 1024
C = 128
HEADS = 4
WIDTH = 32
NX, NZ, NY = 4, 8, 2
DAP = NX * NZ * NY
ROWS = N // DAP
COLS = N // (DAP * HEADS)
TILE = 256
LOG2E = math.log2(math.e)
PENALTY = -2.0 * LOG2E
MASKED = -1e9 * LOG2E
NT = (((1,), (1,)), ((), ()))
TN = (((0,), (0,)), ((), ()))


def dot(a, b, dims=(((1,), (0,)), ((), ()))):
    return lax.dot_general(a, b, dims, preferred_element_type=f32)


def norm_kernel(head_ref, pair_ref, normed_ref, send_ref):
    x = pair_ref[0].astype(f32)
    mean = jnp.mean(x, -1, keepdims=True)
    centered = x - mean
    variance = jnp.mean(centered * centered, -1, keepdims=True)
    normed_ref[0] = (centered * lax.rsqrt(variance + 1e-05)).astype(bf16)
    for c in range(COLS):
        start = pl.multiple_of(c * HEADS * DAP + head_ref[0] * DAP, DAP)
        send_ref[c, 0] = normed_ref[0, pl.ds(start, DAP), :]


def norm_call(pair, head):
    return pl.pallas_call(
        norm_kernel,
        grid_spec=pltpu.PrefetchScalarGridSpec(
            num_scalar_prefetch=1,
            grid=(ROWS,),
            in_specs=[pl.BlockSpec((1, N, C), lambda r, h: (r, 0, 0))],
            out_specs=[
                pl.BlockSpec((1, N, C), lambda r, h: (r, 0, 0)),
                pl.BlockSpec((COLS, 1, DAP, C), lambda r, h: (0, r, 0, 0)),
            ],
        ),
        out_shape=[
            jax.ShapeDtypeStruct((ROWS, N, C), bf16),
            jax.ShapeDtypeStruct((COLS, ROWS, DAP, C), bf16),
        ],
        name="norm",
    )(head, pair)


def bias_kernel(normed_ref, w_ref, out_ref):
    rows = normed_ref.shape[0]
    for r in range(rows):
        b = dot(w_ref[...], normed_ref[r], NT)
        out_ref[0, pl.ds(r, 1), :] = b[0:1].astype(bf16)
        out_ref[1, pl.ds(r, 1), :] = b[1:2].astype(bf16)


def bias_call(normed, w_two):
    return pl.pallas_call(
        bias_kernel,
        in_specs=[pl.BlockSpec(memory_space=pltpu.VMEM)] * 2,
        out_specs=pl.BlockSpec(memory_space=pltpu.VMEM),
        out_shape=jax.ShapeDtypeStruct((2, ROWS, N), bf16),
        compiler_params=pltpu.CompilerParams(vmem_limit_bytes=32 * 2**20),
        name="bias",
    )(normed, w_two)


def attend_kernel(
    x_ref, recv_ref, keep_ref, chain_col_ref, chain_row_ref, w_ref, wout_ref,
    b0, b1, b2, b3, b4, b5, b6, b7, out_ref, k_scr, q_scr, v_scr, g_scr, comb, s_scr, gated,
):
    pieces = ((b0, b1, b2, b3), (b4, b5, b6, b7))
    tile = pl.program_id(0)
    chunk_rows = N // NX
    per_chunk = DAP // NX

    @pl.when(tile == 0)
    def _():
        def project(c, carry):
            whole = recv_ref[:, c].reshape(N, C)
            q = (dot(w_ref[0].reshape(C, C), whole, NT) * WIDTH ** (-0.5)).astype(bf16)
            q = q.astype(f32) * LOG2E
            high = q.astype(bf16)
            low = (q - high.astype(f32)).astype(bf16)
            for h in range(HEADS):
                at = slice(h * WIDTH, (h + 1) * WIDTH)
                q_scr[c, h, 0:WIDTH] = high[at]
                q_scr[c, h, WIDTH : 2 * WIDTH] = low[at]
            gate = jax.nn.sigmoid(dot(w_ref[3].reshape(C, C), whole, NT))
            g_scr[c] = gate.astype(bf16)
            for s in range(NX):
                part = lax.rem(x_ref[0] + s, NX)
                rows = recv_ref[pl.ds(part * per_chunk, per_chunk), c].reshape(chunk_rows, C)
                here = pl.ds(s * chunk_rows, chunk_rows)
                for p in range(2):
                    wk = jnp.concatenate(
                        [w_ref[1, 2 * p], w_ref[1, 2 * p], w_ref[1, 2 * p + 1], w_ref[1, 2 * p + 1]], 0
                    )
                    k_scr[p, c, here] = (dot(rows, wk, NT) * keep_ref[part]).astype(bf16)
                v = dot(w_ref[2].reshape(C, C), rows, NT).astype(bf16)
                ones = jnp.where(
                    lax.broadcasted_iota(jnp.int32, (16, chunk_rows), 0) == 0, 1.0, 0.0
                ).astype(bf16)
                for h in range(HEADS):
                    v_scr[c, h, 0:WIDTH, here] = v[h * WIDTH : (h + 1) * WIDTH]
                    v_scr[c, h, WIDTH : WIDTH + 16, here] = ones
            return carry

        lax.fori_loop(0, COLS, project, 0)

    lanes = pl.ds(pl.multiple_of(tile * TILE, TILE), TILE)
    zeros = jnp.zeros((2 * WIDTH, TILE), bf16)
    for h in range(HEADS):
        for s in range(NX):
            part = lax.rem(x_ref[0] + s, NX)
            same = chain_col_ref[part] == chain_row_ref[0:1, :]
            term = pieces[h // 2][s][h % 2].astype(f32) * LOG2E + jnp.where(same, 0.0, PENALTY)
            comb[s] = jnp.where(keep_ref[part] > 0, term, MASKED)

        def column(c, carry, h=h):
            q = q_scr[c, h, :, lanes]
            q = jnp.concatenate([q, zeros] if h % 2 == 0 else [zeros, q], 0)
            top = None
            for s in range(NX):
                k = k_scr[h // 2, c, pl.ds(s * chunk_rows, chunk_rows)]
                scores = dot(k, q) + comb[s]
                s_scr[s] = scores
                high = jnp.max(scores.reshape(chunk_rows // 8, 8, TILE), 0)
                top = high if top is None else jnp.maximum(top, high)
            top = jnp.max(top, 0, keepdims=True)
            total = jnp.zeros((WIDTH + 16, TILE), f32)
            for s in range(NX):
                weights = jnp.exp2(s_scr[s] - top).astype(bf16)
                total = total + dot(v_scr[c, h, :, pl.ds(s * chunk_rows, chunk_rows)], weights)
            attended = (total[0:WIDTH] / total[WIDTH : WIDTH + 1]).astype(bf16).astype(f32)
            gate = g_scr[c, h * WIDTH : (h + 1) * WIDTH, lanes].astype(f32)
            gated[c, h * WIDTH : (h + 1) * WIDTH] = (gate * attended).astype(bf16)
            return carry

        lax.fori_loop(0, COLS, column, 0)
    joined = gated[...].reshape(COLS * C, TILE)
    for o in range(HEADS):
        out_ref[o] = dot(joined, wout_ref[o], TN).astype(bf16)


def attend_call(x, recv, keep, chain_col, chain_row, weights, w_out, pieces):
    whole = lambda shape: pl.BlockSpec(shape, lambda t, x: (0,) * len(shape))
    return pl.pallas_call(
        attend_kernel,
        grid_spec=pltpu.PrefetchScalarGridSpec(
            num_scalar_prefetch=1,
            grid=(N // TILE,),
            in_specs=[
                whole((DAP, COLS, ROWS, C)),
                whole((NX, N // NX, 1)),
                whole((NX, N // NX, 1)),
                pl.BlockSpec((8, TILE), lambda t, x: (0, t)),
                whole((4, HEADS, WIDTH, C)),
                whole((HEADS, COLS * C, C)),
            ]
            + [pl.BlockSpec((2, N // NX, TILE), lambda t, x: (0, 0, t))] * 8,
            out_specs=pl.BlockSpec((HEADS, TILE, C), lambda t, x: (0, t, 0)),
            scratch_shapes=[
                pltpu.VMEM((2, COLS, N, C), bf16),
                pltpu.VMEM((COLS, HEADS, 2 * WIDTH, N), bf16),
                pltpu.VMEM((COLS, HEADS, WIDTH + 16, N), bf16),
                pltpu.VMEM((COLS, C, N), bf16),
                pltpu.VMEM((NX, N // NX, TILE), f32),
                pltpu.VMEM((NX, N // NX, TILE), f32),
                pltpu.VMEM((COLS, C, TILE), bf16),
            ],
        ),
        out_shape=jax.ShapeDtypeStruct((HEADS, N, C), bf16),
        compiler_params=pltpu.CompilerParams(vmem_limit_bytes=48 * 2**20),
        name="attend",
    )(x, recv, keep, chain_col, chain_row, weights, w_out, *pieces)


def at(x, z, y):
    return (x % NX) * NZ * NY + (z % NZ) * NY + y % NY


def shift(dx, dz, dy):
    return [
        (at(x, z, y), at(x + dx, z + dz, y + dy))
        for x in range(NX) for z in range(NZ) for y in range(NY)
    ]


def send(value, dx, dz, dy):
    return lax.ppermute(value, "dap", shift(dx, dz, dy))


def gather_plane(rows, z, y):
    other = send(rows, 0, 0, 1)
    first = jnp.where(y == 0, rows, other)
    second = jnp.where(y == 0, other, rows)
    mine = jnp.concatenate([first, second], 1)
    up = down = mine
    got = {0: mine}
    for step in range(1, 4):
        up, down = send(up, 0, 1, 0), send(down, 0, -1, 0)
        got[NZ - step], got[step] = up, down
    got[4] = jnp.concatenate([send(up[:1], 0, 1, 0), send(down[1:], 0, -1, 0)], 0)
    ordered = jnp.concatenate([got[i] for i in range(NZ)] * 2, 1)
    start = (NZ - z) % NZ * (NY * ROWS)
    return lax.dynamic_slice_in_dim(ordered, start, NZ * NY * ROWS, 1)


def gather_bias(rows, z, y):
    plane = gather_plane(rows, z, y)
    left, right = send(plane, 1, 0, 0), send(plane, -1, 0, 0)
    far = jnp.concatenate([send(left[:1], 1, 0, 0), send(right[1:], -1, 0, 0)], 0)
    own = [plane, right, far, left]
    swap = [(h, h ^ 1) for h in range(HEADS)]
    return own + [lax.ppermute(piece, "head", swap) for piece in own]


def body(pair, residue_mask, chain_breaks, w_query, w_key, w_value, w_gate, w_bias, w_out):
    dap = lax.axis_index("dap").astype(jnp.int32)
    head = lax.axis_index("head").astype(jnp.int32)
    x, z, y = dap // (NZ * NY), dap // NY % NZ, dap % NY
    core = head % 2
    packed = jnp.concatenate(
        [w_query.T, w_key.T, w_value.T, w_gate.T, w_out, w_bias.T, jnp.zeros((15, C), bf16)], 0
    )
    packed = lax.all_gather(packed, "head", axis=0)
    packed = lax.dynamic_slice_in_dim(jnp.concatenate([packed, packed], 0), 2 * core, HEADS, 0)
    weights = jnp.swapaxes(packed[:, : 4 * WIDTH].reshape(HEADS, 4, WIDTH, C), 0, 1)
    full_out = packed[:, 4 * WIDTH : 5 * WIDTH].reshape(C, HEADS, WIDTH)
    eye = jnp.eye(COLS, dtype=bf16)
    spread = (
        jnp.transpose(full_out, (1, 0, 2))[:, None, :, None, :] * eye[None, :, None, :, None]
    ).reshape(HEADS, COLS * C, COLS * WIDTH)
    w_two = packed[:2, 5 * WIDTH]
    w_two = jnp.concatenate([w_two, jnp.zeros((14, C), bf16)], 0)

    normed, out = norm_call(pair, head[None])
    recv = lax.all_to_all(jnp.transpose(out, (2, 0, 1, 3)), "dap", 0, 0, tiled=True)
    pieces = gather_bias(bias_call(normed, w_two), z, y)

    chain = jnp.cumsum(chain_breaks).astype(jnp.int32)
    keep = (residue_mask > 0).astype(f32).reshape(NX, N // NX, 1)
    update = attend_call(
        x[None], recv, keep, chain.reshape(NX, N // NX, 1),
        jnp.broadcast_to(chain[None], (8, N)), weights, spread, pieces,
    )
    update = update.reshape(HEADS * DAP, ROWS, C)
    update = lax.all_to_all(update, ("head", "dap"), 0, 0, tiled=True)
    update = update.reshape(HEADS * DAP, ROWS, COLS, WIDTH)
    return jnp.transpose(update, (1, 2, 0, 3)).reshape(ROWS, N, WIDTH)


def solution(mesh):
    placed = (
        P("dap", None, None), P(), P(),
        P(None, "head"), P(None, "head"), P(None, "head"), P(None, "head"), P(None, "head"),
        P("head", None),
    )
    return jax.shard_map(
        body, mesh=mesh, in_specs=placed, out_specs=P("dap", None, "head"), check_vma=False
    )
```

```python
import functools
import math

import jax
import jax.numpy as jnp
from jax import lax
from jax.experimental import pallas as pl
from jax.experimental.pallas import tpu as pltpu
from jax.sharding import PartitionSpec as P

bf16 = jnp.bfloat16
f32 = jnp.float32

N = 1024
C = 128
HEADS = 4
WIDTH = 32
NX, NZ, NY = 4, 8, 2
DAP = NX * NZ * NY
ROWS = N // DAP
COLS = N // (DAP * HEADS)
TILE = 256
LOG2E = math.log2(math.e)
PENALTY = -2.0
MASKED = -1e9
NT = (((1,), (1,)), ((), ()))
TN = (((0,), (0,)), ((), ()))


def dot(a, b, dims=(((1,), (0,)), ((), ()))):
    return lax.dot_general(a, b, dims, preferred_element_type=f32)


def norm_kernel(head_ref, pair_ref, normed_ref, send_ref):
    average = jnp.full((C, C), 1.0 / C, bf16)
    twice = jnp.full((2 * C, C), 1.0 / C, bf16)
    for r in range(pair_ref.shape[0]):
        x = pair_ref[r]
        centered = x.astype(f32) - dot(x, average)
        square = centered * centered
        high = square.astype(bf16)
        low = (square - high.astype(f32)).astype(bf16)
        variance = dot(jnp.concatenate([high, low], 1), twice)
        normed_ref[r] = (centered * lax.rsqrt(variance + 1e-05)).astype(bf16)
        for c in range(COLS):
            start = pl.multiple_of(c * HEADS * DAP + head_ref[0] * DAP, DAP)
            send_ref[c, r] = normed_ref[r, pl.ds(start, DAP), :]


def norm_call(pair, head):
    step = 4
    return pl.pallas_call(
        norm_kernel,
        grid_spec=pltpu.PrefetchScalarGridSpec(
            num_scalar_prefetch=1,
            grid=(ROWS // step,),
            in_specs=[pl.BlockSpec((step, N, C), lambda r, h: (r, 0, 0))],
            out_specs=[
                pl.BlockSpec((step, N, C), lambda r, h: (r, 0, 0)),
                pl.BlockSpec((COLS, step, DAP, C), lambda r, h: (0, r, 0, 0)),
            ],
        ),
        out_shape=[
            jax.ShapeDtypeStruct((ROWS, N, C), bf16),
            jax.ShapeDtypeStruct((COLS, ROWS, DAP, C), bf16),
        ],
        cost_estimate=cost(6, 9 * 2**20),
        compiler_params=pltpu.CompilerParams(vmem_limit_bytes=32 * 2**20),
        name="norm",
    )(head, pair)


def cost(us, moved=0):
    return pl.CostEstimate(flops=int(us * 1.1e9), bytes_accessed=moved, transcendentals=0)


def bias_kernel(normed_ref, w_ref, out_ref):
    rows = normed_ref.shape[0]
    for r in range(rows):
        b = dot(w_ref[...], normed_ref[r], NT)
        out_ref[0, pl.ds(r, 1), :] = b[0:1].astype(bf16)
        out_ref[1, pl.ds(r, 1), :] = b[1:2].astype(bf16)


def bias_call(normed, w_two):
    return pl.pallas_call(
        bias_kernel,
        in_specs=[pl.BlockSpec(memory_space=pltpu.VMEM)] * 2,
        out_specs=pl.BlockSpec(memory_space=pltpu.VMEM),
        out_shape=jax.ShapeDtypeStruct((2, ROWS, N), bf16),
        cost_estimate=cost(1.5),
        compiler_params=pltpu.CompilerParams(vmem_limit_bytes=32 * 2**20),
        name="bias",
    )(normed, w_two)


def pack_kernel(wq, wk, wv, wg, wo, out_ref):
    for n, ref in enumerate((wq, wk, wv, wg, wo)):
        out_ref[n] = ref[...]


def pack_call(*weights):
    return pl.pallas_call(
        pack_kernel,
        in_specs=[pl.BlockSpec(memory_space=pltpu.VMEM)] * 5,
        out_specs=pl.BlockSpec(memory_space=pltpu.VMEM),
        out_shape=jax.ShapeDtypeStruct((5, WIDTH, C), bf16),
        cost_estimate=cost(1),
        name="pack",
    )(*weights)


def mask_kernel(place_ref, mask_ref, breaks_ref, extra_ref, keep_ref):
    chunk = N // NX
    row = breaks_ref[0:1, :].astype(f32)
    ones = jnp.ones((C, N), f32)
    breaks = (ones * row).astype(bf16)
    mask = (ones * (mask_ref[0:1, :] > 0).astype(f32)).astype(bf16)
    before = (
        lax.broadcasted_iota(jnp.int32, (N, N), 0) <= lax.broadcasted_iota(jnp.int32, (N, N), 1)
    )
    chain_row = dot(breaks[:16], jnp.where(before, 1.0, 0.0).astype(bf16))[0:1]
    for s in range(NX):
        k = jnp.concatenate(
            [
                lax.broadcasted_iota(jnp.int32, (ROWS, N), 0) + dap_of(place_ref, s, n, t) * ROWS
                for n in range(NZ) for t in range(NY)
            ],
            0,
        )
        j = lax.broadcasted_iota(jnp.int32, (chunk, N), 1)
        chain = dot(jnp.where(j <= k, 1.0, 0.0).astype(bf16), breaks, NT)
        keep = dot(jnp.where(j == k, 1.0, 0.0).astype(bf16), mask, NT)
        keep_ref[s] = keep.astype(bf16)
        for t in range(N // C):
            at = slice(t * C, (t + 1) * C)
            value = jnp.where(chain == chain_row[:, at], 0.0, PENALTY)
            extra_ref[s, :, at] = jnp.where(keep > 0.5, value, MASKED).astype(bf16)


def mask_call(place, mask, breaks):
    return pl.pallas_call(
        mask_kernel,
        in_specs=[pl.BlockSpec(memory_space=pltpu.SMEM)] + [pl.BlockSpec(memory_space=pltpu.VMEM)] * 2,
        out_specs=[pl.BlockSpec(memory_space=pltpu.VMEM)] * 2,
        out_shape=[
            jax.ShapeDtypeStruct((NX, N // NX, N), bf16),
            jax.ShapeDtypeStruct((NX, N // NX, C), bf16),
        ],
        cost_estimate=cost(2),
        compiler_params=pltpu.CompilerParams(vmem_limit_bytes=32 * 2**20),
        name="mask",
    )(place, mask, breaks)


def order_weights(upper_ref, parts, w_ref, spread_ref):
    for h in range(HEADS):
        low, high = parts[h // 2 * 2], parts[h // 2 * 2 + 1]
        w_ref[h] = jnp.where(upper_ref[0] == h % 2, low[...], high[...])
    w_out = jnp.concatenate([w_ref[h, 4] for h in range(HEADS)], 0)
    a = lax.broadcasted_iota(jnp.int32, (C, C), 0)
    b = lax.broadcasted_iota(jnp.int32, (C, C), 1)
    for o in range(HEADS):
        for c in range(COLS):
            pick = (b // WIDTH == c) & (a == b - c * WIDTH + o * WIDTH)
            moved = dot(w_out, jnp.where(pick, 1.0, 0.0).astype(bf16))
            spread_ref[o, c * C : (c + 1) * C] = moved.astype(bf16)


AROUND = (0, -1, 1, -2, 2, -3, 3, 4)


def dap_of(place_ref, s, n, t):
    x, z, y = place_ref[0], place_ref[1], place_ref[2]
    return ((x + s) & (NX - 1)) * (NZ * NY) + ((z + NZ + AROUND[n]) & (NZ - 1)) * NY + (y ^ t)


def project(c, place_ref, recv_ref, keep_ref, w_ref, k_ref, q_ref, v_ref, g_ref):
    chunk = N // NX
    weight = lambda n: w_ref[:, n].reshape(C, C)
    whole = recv_ref[:, c].reshape(N, C)
    q = (dot(weight(0), whole, NT) * WIDTH ** (-0.5)).astype(bf16)
    q = q.astype(f32) * LOG2E
    high = q.astype(bf16)
    low = (q - high.astype(f32)).astype(bf16)
    for h in range(HEADS):
        rows = slice(h * WIDTH, (h + 1) * WIDTH)
        q_ref[c, h, 0:WIDTH] = high[rows]
        q_ref[c, h, WIDTH : 2 * WIDTH] = low[rows]
    g_ref[c] = jax.nn.sigmoid(dot(weight(3), whole, NT)).astype(bf16)
    ones = jnp.where(lax.broadcasted_iota(jnp.int32, (16, chunk), 0) == 0, 1.0, 0.0).astype(bf16)
    for s in range(NX):
        rows = jnp.concatenate(
            [recv_ref[dap_of(place_ref, s, n, t), c] for n in range(NZ) for t in range(NY)], 0
        )
        here = slice(s * chunk, (s + 1) * chunk)
        for p in range(2):
            first, second = w_ref[2 * p, 1], w_ref[2 * p + 1, 1]
            wk = jnp.concatenate([first, first, second, second], 0)
            k_ref[c, p, here] = dot(rows, wk, NT).astype(bf16) * keep_ref[s]
        v = dot(weight(2), rows, NT).astype(bf16)
        for h in range(HEADS):
            v_ref[c, h, 0:WIDTH, here] = v[h * WIDTH : (h + 1) * WIDTH]
            v_ref[c, h, WIDTH : WIDTH + 16, here] = ones


def attend_kernel(
    place_ref, upper_ref, recv_ref, keep_ref, extra_ref, *rest
):
    parts, bias_refs = rest[:4], rest[4:24]
    out_ref, w_ref, wout_ref, k_ref, q_ref, v_ref, g_ref, comb, s_scr, gated = rest[24:]
    lanes = pl.ds(pl.multiple_of(pl.program_id(0) * TILE, TILE), TILE)

    @pl.when(pl.program_id(0) == 0)
    def _():
        order_weights(upper_ref, parts, w_ref, wout_ref)

        def step(c, carry):
            project(c, place_ref, recv_ref, keep_ref, w_ref, k_ref, q_ref, v_ref, g_ref)
            return carry

        lax.fori_loop(0, COLS, step, 0)

    chunk = N // NX
    zeros = jnp.zeros((2 * WIDTH, TILE), bf16)

    def bias(h, s):
        parts = bias_refs[10 * (h // 2) : 10 * (h // 2) + 10]
        if s == 2:
            return [parts[2 + 5 * group + h % 2][0] for group in range(2)]
        return [parts[(0, 1, None, 4)[s] + 5 * group][h % 2] for group in range(2)]

    def score(h, c, s, q, top):
        k = k_ref[c, h // 2, s * chunk : (s + 1) * chunk]
        scores = dot(k, q) + comb[h % 2, s]
        s_scr[c % 2, s] = scores
        high = jnp.max(scores.reshape(chunk // 8, 8, TILE), 0)
        return high if top is None else jnp.maximum(top, high)

    def weigh(h, c, s, top, total):
        weights = jnp.exp2(s_scr[c % 2, s] - top).astype(bf16)
        part = dot(v_ref[c, h, :, s * chunk : (s + 1) * chunk], weights)
        return part if total is None else total + part

    def finish(h, c, total):
        attended = (total[0:WIDTH] / total[WIDTH : WIDTH + 1]).astype(bf16).astype(f32)
        rows = slice(h * WIDTH, (h + 1) * WIDTH)
        gated[c, rows] = (g_ref[c, rows, lanes].astype(f32) * attended).astype(bf16)

    steps = [(h, c) for h in range(HEADS) for c in range(COLS)]
    before = None
    for h, c in steps + [(None, None)]:
        if h is not None:
            if c == 0:
                for s in range(NX):
                    start = 0
                    for part in bias(h, s):
                        here = slice(start, start + part.shape[0])
                        extra = extra_ref[s, here].astype(f32)
                        value = jnp.where(extra > 0.5 * MASKED, part.astype(f32) + extra, MASKED)
                        comb[h % 2, s, here] = value * LOG2E
                        start += part.shape[0]
            q = q_ref[c, h, :, lanes]
            q = jnp.concatenate([q, zeros] if h % 2 == 0 else [zeros, q], 0)
        top = total = None
        for s in range(NX):
            if h is not None:
                top = score(h, c, s, q, top)
            if before is not None:
                total = weigh(before[0], before[1], s, before[2], total)
        if before is not None:
            finish(before[0], before[1], total)
        if h is not None:
            before = (h, c, jnp.max(top, 0, keepdims=True))
    joined = gated[...].reshape(COLS * C, TILE)
    for o in range(HEADS):
        out_ref[o] = dot(joined, wout_ref[o], TN).astype(bf16)


def attend_call(place, upper, recv, keep, extra, parts, pieces):
    whole = lambda shape: pl.BlockSpec(shape, lambda t: (0,) * len(shape))
    along = lambda shape: pl.BlockSpec(shape, lambda t: (0,) * (len(shape) - 1) + (t,))
    return pl.pallas_call(
        attend_kernel,
        grid=(N // TILE,),
        in_specs=[
            pl.BlockSpec(memory_space=pltpu.SMEM),
            pl.BlockSpec(memory_space=pltpu.SMEM),
            whole((DAP, COLS, ROWS, C)),
            whole((NX, N // NX, C)),
            along((NX, N // NX, TILE)),
        ]
        + [whole((5, WIDTH, C))] * 4
        + [along(piece.shape[:2] + (TILE,)) for piece in pieces],
        out_specs=pl.BlockSpec((HEADS, TILE, C), lambda t: (0, t, 0)),
        scratch_shapes=[
            pltpu.VMEM((HEADS, 5, WIDTH, C), bf16),
            pltpu.VMEM((HEADS, COLS * C, C), bf16),
            pltpu.VMEM((COLS, 2, N, C), bf16),
            pltpu.VMEM((COLS, HEADS, 2 * WIDTH, N), bf16),
            pltpu.VMEM((COLS, HEADS, WIDTH + 16, N), bf16),
            pltpu.VMEM((COLS, C, N), bf16),
            pltpu.VMEM((2, NX, N // NX, TILE), f32),
            pltpu.VMEM((2, NX, N // NX, TILE), f32),
            pltpu.VMEM((COLS, C, TILE), bf16),
        ],
        out_shape=jax.ShapeDtypeStruct((HEADS, N, C), bf16),
        cost_estimate=cost(40),
        compiler_params=pltpu.CompilerParams(vmem_limit_bytes=60 * 2**20),
        name="attend",
    )(place, upper, recv, keep, extra, *parts, *pieces)


def at(x, z, y, head):
    return (((x % NX) * NZ + z % NZ) * NY + y % NY) * HEADS + head


def send(value, dx, dz, dy=0):
    pairs = [
        (at(x, z, y, head), at(x + dx, z + dz, y + dy, head ^ (2 * dy)))
        for x in range(NX) for z in range(NZ) for y in range(NY) for head in range(HEADS)
    ]
    return lax.ppermute(value, ("dap", "head"), pairs)


def gather_bias(rows, out):
    beside = send(rows, 0, 0, 1)
    up = jnp.concatenate([send(rows, 0, 1), send(rows, 0, 1, 1)], 1)
    down = jnp.concatenate([send(rows, 0, -1), send(rows, 0, -1, 1)], 1)
    near = jnp.concatenate([rows, beside, up, down], 1)
    got = []
    for step in range(2, 4):
        up, down = send(up, 0, 1), send(down, 0, -1)
        got += [up, down]
    last = [send(up[:1], 0, 1), send(down[1:], 0, -1)]
    out, *last = lax.optimization_barrier((out, *last))
    last = jnp.concatenate(last, 0)
    far = jnp.concatenate(got + [last], 1)
    own = []
    for group in (near, far):
        left, right = send(group, 1, 0), send(group, -1, 0)
        own += [group, right, send(left[:1], 1, 0), send(right[1:], -1, 0), left]
    swap = [(h, h ^ 1) for h in range(HEADS)]
    return own + [lax.ppermute(piece, "head", swap) for piece in own], out


def body(pair, residue_mask, chain_breaks, w_query, w_key, w_value, w_gate, w_bias, w_out):
    dap = lax.axis_index("dap").astype(jnp.int32)
    head = lax.axis_index("head").astype(jnp.int32)
    place = jnp.stack([dap // (NZ * NY), (dap // NY) & (NZ - 1), dap & (NY - 1)])
    w_own = w_bias.T
    w_other = lax.ppermute(w_own, "head", [(h, h ^ 2) for h in range(HEADS)])
    upper = head >= 2
    w_two = jnp.concatenate(
        [jnp.where(upper, w_other, w_own), jnp.where(upper, w_own, w_other), jnp.zeros((14, C), bf16)], 0
    )
    mine = pack_call(w_query.T, w_key.T, w_value.T, w_gate.T, w_out)
    parts = [mine] + [lax.ppermute(mine, "head", [(h, h ^ n) for h in range(HEADS)]) for n in (2, 1, 3)]
    wide = lambda v: jnp.broadcast_to(v[None], (8, N))
    extra, keep = mask_call(place, wide(residue_mask), wide(chain_breaks))
    which, extra, keep = lax.optimization_barrier((head[None], extra, keep))
    normed, out = norm_call(pair, which)
    pieces, out = gather_bias(bias_call(normed, w_two), jnp.transpose(out, (2, 0, 1, 3)))
    recv = lax.all_to_all(out, "dap", 0, 0, tiled=True)
    update = attend_call(place, (head >> 1)[None], recv, keep, extra, parts, pieces)
    update = update.reshape(HEADS * DAP, ROWS, C)
    update = lax.all_to_all(update, ("head", "dap"), 0, 0, tiled=True)
    update = update.reshape(HEADS * DAP, ROWS, COLS, WIDTH)
    return jnp.transpose(update, (1, 2, 0, 3)).reshape(ROWS, N, WIDTH)


def solution(mesh):
    placed = (
        P("dap", None, None), P(), P(),
        P(None, "head"), P(None, "head"), P(None, "head"), P(None, "head"), P(None, "head"),
        P("head", None),
    )
    return jax.shard_map(
        body, mesh=mesh, in_specs=placed, out_specs=P("dap", None, "head"), check_vma=False
    )
```

```python
import functools
import math

import jax
import jax.numpy as jnp
from jax import lax
from jax.experimental import pallas as pl
from jax.experimental.pallas import tpu as pltpu
from jax.sharding import PartitionSpec as P

bf16 = jnp.bfloat16
f32 = jnp.float32

N = 1024
C = 128
HEADS = 4
WIDTH = 32
NX, NZ, NY = 4, 8, 2
DAP = NX * NZ * NY
ROWS = N // DAP
COLS = N // (DAP * HEADS)
TILE = 512
LOG2E = math.log2(math.e)
PENALTY = -2.0
MASKED = -1e9
NT = (((1,), (1,)), ((), ()))
TN = (((0,), (0,)), ((), ()))


def dot(a, b, dims=(((1,), (0,)), ((), ()))):
    return lax.dot_general(a, b, dims, preferred_element_type=f32)


def norm_kernel(head_ref, pair_ref, normed_ref, send_ref):
    average = jnp.full((C, C), 1.0 / C, bf16)
    twice = jnp.full((2 * C, C), 1.0 / C, bf16)
    for r in range(pair_ref.shape[0]):
        x = pair_ref[r]
        centered = x.astype(f32) - dot(x, average)
        square = centered * centered
        high = square.astype(bf16)
        low = (square - high.astype(f32)).astype(bf16)
        variance = dot(jnp.concatenate([high, low], 1), twice)
        normed_ref[r] = (centered * lax.rsqrt(variance + 1e-05)).astype(bf16)
        for c in range(COLS):
            start = pl.multiple_of(c * HEADS * DAP + head_ref[0] * DAP, DAP)
            send_ref[c, r] = normed_ref[r, pl.ds(start, DAP), :]


def norm_call(pair, head):
    step = 4
    return pl.pallas_call(
        norm_kernel,
        grid_spec=pltpu.PrefetchScalarGridSpec(
            num_scalar_prefetch=1,
            grid=(ROWS // step,),
            in_specs=[pl.BlockSpec((step, N, C), lambda r, h: (r, 0, 0))],
            out_specs=[
                pl.BlockSpec((step, N, C), lambda r, h: (r, 0, 0)),
                pl.BlockSpec((COLS, step, DAP, C), lambda r, h: (0, r, 0, 0)),
            ],
        ),
        out_shape=[
            jax.ShapeDtypeStruct((ROWS, N, C), bf16),
            jax.ShapeDtypeStruct((COLS, ROWS, DAP, C), bf16),
        ],
        cost_estimate=cost(6, 9 * 2**20),
        compiler_params=pltpu.CompilerParams(vmem_limit_bytes=32 * 2**20),
        name="norm",
    )(head, pair)


def cost(us, moved=0):
    return pl.CostEstimate(flops=int(us * 1.1e9), bytes_accessed=moved, transcendentals=0)


def bias_kernel(normed_ref, w_ref, out_ref):
    rows = normed_ref.shape[0]
    for r in range(rows):
        b = dot(w_ref[...], normed_ref[r], NT)
        out_ref[0, pl.ds(r, 1), :] = b[0:1].astype(bf16)
        out_ref[1, pl.ds(r, 1), :] = b[1:2].astype(bf16)


def bias_call(normed, w_two):
    return pl.pallas_call(
        bias_kernel,
        in_specs=[pl.BlockSpec(memory_space=pltpu.VMEM)] * 2,
        out_specs=pl.BlockSpec(memory_space=pltpu.VMEM),
        out_shape=jax.ShapeDtypeStruct((2, ROWS, N), bf16),
        cost_estimate=cost(1.5),
        compiler_params=pltpu.CompilerParams(vmem_limit_bytes=32 * 2**20),
        name="bias",
    )(normed, w_two)


def pack_kernel(wq, wk, wv, wg, wo, out_ref):
    for n, ref in enumerate((wq, wk, wv, wg, wo)):
        out_ref[n] = ref[...]


def pack_call(*weights):
    return pl.pallas_call(
        pack_kernel,
        in_specs=[pl.BlockSpec(memory_space=pltpu.VMEM)] * 5,
        out_specs=pl.BlockSpec(memory_space=pltpu.VMEM),
        out_shape=jax.ShapeDtypeStruct((5, WIDTH, C), bf16),
        cost_estimate=cost(1),
        name="pack",
    )(*weights)


def mask_kernel(place_ref, mask_ref, breaks_ref, extra_ref, keep_ref):
    chunk = N // NX
    row = breaks_ref[0:1, :].astype(f32)
    ones = jnp.ones((C, N), f32)
    breaks = (ones * row).astype(bf16)
    mask = (ones * (mask_ref[0:1, :] > 0).astype(f32)).astype(bf16)
    before = (
        lax.broadcasted_iota(jnp.int32, (N, N), 0) <= lax.broadcasted_iota(jnp.int32, (N, N), 1)
    )
    chain_row = dot(breaks[:16], jnp.where(before, 1.0, 0.0).astype(bf16))[0:1]
    for s in range(NX):
        k = jnp.concatenate(
            [
                lax.broadcasted_iota(jnp.int32, (ROWS, N), 0) + dap_of(place_ref, s, n, t) * ROWS
                for n in range(NZ) for t in range(NY)
            ],
            0,
        )
        j = lax.broadcasted_iota(jnp.int32, (chunk, N), 1)
        chain = dot(jnp.where(j <= k, 1.0, 0.0).astype(bf16), breaks, NT)
        keep = dot(jnp.where(j == k, 1.0, 0.0).astype(bf16), mask, NT)
        keep_ref[s] = keep.astype(bf16)
        for t in range(N // C):
            at = slice(t * C, (t + 1) * C)
            value = jnp.where(chain == chain_row[:, at], 0.0, PENALTY)
            extra_ref[s, :, at] = jnp.where(keep > 0.5, value, MASKED).astype(bf16)


def mask_call(place, mask, breaks):
    return pl.pallas_call(
        mask_kernel,
        in_specs=[pl.BlockSpec(memory_space=pltpu.SMEM)] + [pl.BlockSpec(memory_space=pltpu.VMEM)] * 2,
        out_specs=[pl.BlockSpec(memory_space=pltpu.VMEM)] * 2,
        out_shape=[
            jax.ShapeDtypeStruct((NX, N // NX, N), bf16),
            jax.ShapeDtypeStruct((NX, N // NX, C), bf16),
        ],
        cost_estimate=cost(2),
        compiler_params=pltpu.CompilerParams(vmem_limit_bytes=32 * 2**20),
        name="mask",
    )(place, mask, breaks)


def order_weights(upper_ref, parts, w_ref, spread_ref):
    for h in range(HEADS):
        low, high = parts[h // 2 * 2], parts[h // 2 * 2 + 1]
        w_ref[h] = jnp.where(upper_ref[0] == h % 2, low[...], high[...])
    w_out = jnp.concatenate([w_ref[h, 4] for h in range(HEADS)], 0)
    a = lax.broadcasted_iota(jnp.int32, (C, C), 0)
    b = lax.broadcasted_iota(jnp.int32, (C, C), 1)
    for o in range(HEADS):
        for c in range(COLS):
            pick = (b // WIDTH == c) & (a == b - c * WIDTH + o * WIDTH)
            moved = dot(w_out, jnp.where(pick, 1.0, 0.0).astype(bf16))
            spread_ref[o, c * C : (c + 1) * C] = moved.astype(bf16)


AROUND = (0, -1, 1, -2, 2, -3, 3, 4)


def dap_of(place_ref, s, n, t):
    x, z, y = place_ref[0], place_ref[1], place_ref[2]
    return ((x + s) & (NX - 1)) * (NZ * NY) + ((z + NZ + AROUND[n]) & (NZ - 1)) * NY + (y ^ t)


def project(c, place_ref, recv_ref, keep_ref, w_ref, k_ref, q_ref, v_ref, g_ref):
    chunk = N // NX
    weight = lambda n: w_ref[:, n].reshape(C, C)
    whole = recv_ref[:, c].reshape(N, C)
    q = (dot(weight(0), whole, NT) * WIDTH ** (-0.5)).astype(bf16)
    q = q.astype(f32) * LOG2E
    high = q.astype(bf16)
    low = (q - high.astype(f32)).astype(bf16)
    for h in range(HEADS):
        rows = slice(h * WIDTH, (h + 1) * WIDTH)
        q_ref[c, h, 0:WIDTH] = high[rows]
        q_ref[c, h, WIDTH : 2 * WIDTH] = low[rows]
    g_ref[c] = jax.nn.sigmoid(dot(weight(3), whole, NT)).astype(bf16)
    ones = jnp.where(lax.broadcasted_iota(jnp.int32, (16, chunk), 0) == 0, 1.0, 0.0).astype(bf16)
    for s in range(NX):
        rows = jnp.concatenate(
            [recv_ref[dap_of(place_ref, s, n, t), c] for n in range(NZ) for t in range(NY)], 0
        )
        here = slice(s * chunk, (s + 1) * chunk)
        for p in range(2):
            first, second = w_ref[2 * p, 1], w_ref[2 * p + 1, 1]
            wk = jnp.concatenate([first, first, second, second], 0)
            k_ref[c, p, here] = dot(rows, wk, NT).astype(bf16) * keep_ref[s]
        v = dot(weight(2), rows, NT).astype(bf16)
        for h in range(HEADS):
            v_ref[c, h, 0:WIDTH, here] = v[h * WIDTH : (h + 1) * WIDTH]
            v_ref[c, h, WIDTH : WIDTH + 16, here] = ones


def attend_kernel(
    place_ref, upper_ref, recv_ref, keep_ref, extra_ref, *rest
):
    parts, bias_refs = rest[:4], rest[4:24]
    out_ref, w_ref, wout_ref, k_ref, q_ref, v_ref, g_ref, comb, s_scr, gated = rest[24:]
    lanes = pl.ds(pl.multiple_of(pl.program_id(0) * TILE, TILE), TILE)

    @pl.when(pl.program_id(0) == 0)
    def _():
        order_weights(upper_ref, parts, w_ref, wout_ref)

        def step(c, carry):
            project(c, place_ref, recv_ref, keep_ref, w_ref, k_ref, q_ref, v_ref, g_ref)
            return carry

        lax.fori_loop(0, COLS, step, 0)

    chunk = N // NX
    zeros = jnp.zeros((2 * WIDTH, TILE), bf16)

    def bias(h, s):
        parts = bias_refs[10 * (h // 2) : 10 * (h // 2) + 10]
        if s == 2:
            return [parts[2 + 5 * group + h % 2][0] for group in range(2)]
        return [parts[(0, 1, None, 4)[s] + 5 * group][h % 2] for group in range(2)]

    def score(h, c, s, q, top):
        k = k_ref[c, h // 2, s * chunk : (s + 1) * chunk]
        scores = dot(k, q) + comb[h % 2, s]
        s_scr[c % 2, s] = scores
        high = jnp.max(scores.reshape(chunk // 8, 8, TILE), 0)
        return high if top is None else jnp.maximum(top, high)

    def weigh(h, c, s, top, total):
        weights = jnp.exp2(s_scr[c % 2, s] - top).astype(bf16)
        part = dot(v_ref[c, h, :, s * chunk : (s + 1) * chunk], weights)
        return part if total is None else total + part

    def finish(h, c, total):
        attended = (total[0:WIDTH] / total[WIDTH : WIDTH + 1]).astype(bf16).astype(f32)
        rows = slice(h * WIDTH, (h + 1) * WIDTH)
        gated[c, rows] = (g_ref[c, rows, lanes].astype(f32) * attended).astype(bf16)

    steps = [(h, c) for h in range(HEADS) for c in range(COLS)]
    before = None
    for h, c in steps + [(None, None)]:
        if h is not None:
            if c == 0:
                for s in range(NX):
                    start = 0
                    for part in bias(h, s):
                        here = slice(start, start + part.shape[0])
                        extra = extra_ref[s, here].astype(f32)
                        value = jnp.where(extra > 0.5 * MASKED, part.astype(f32) + extra, MASKED)
                        comb[h % 2, s, here] = value * LOG2E
                        start += part.shape[0]
            q = q_ref[c, h, :, lanes]
            q = jnp.concatenate([q, zeros] if h % 2 == 0 else [zeros, q], 0)
        top = total = None
        for s in range(NX):
            if h is not None:
                top = score(h, c, s, q, top)
            if before is not None:
                total = weigh(before[0], before[1], s, before[2], total)
        if before is not None:
            finish(before[0], before[1], total)
        if h is not None:
            before = (h, c, jnp.max(top, 0, keepdims=True))
    joined = gated[...].reshape(COLS * C, TILE)
    for o in range(HEADS):
        out_ref[o] = dot(joined, wout_ref[o], TN).astype(bf16)


def attend_call(place, upper, recv, keep, extra, parts, pieces):
    whole = lambda shape: pl.BlockSpec(shape, lambda t: (0,) * len(shape))
    along = lambda shape: pl.BlockSpec(shape, lambda t: (0,) * (len(shape) - 1) + (t,))
    return pl.pallas_call(
        attend_kernel,
        grid=(N // TILE,),
        in_specs=[
            pl.BlockSpec(memory_space=pltpu.SMEM),
            pl.BlockSpec(memory_space=pltpu.SMEM),
            whole((DAP, COLS, ROWS, C)),
            whole((NX, N // NX, C)),
            along((NX, N // NX, TILE)),
        ]
        + [whole((5, WIDTH, C))] * 4
        + [along(piece.shape[:2] + (TILE,)) for piece in pieces],
        out_specs=pl.BlockSpec((HEADS, TILE, C), lambda t: (0, t, 0)),
        scratch_shapes=[
            pltpu.VMEM((HEADS, 5, WIDTH, C), bf16),
            pltpu.VMEM((HEADS, COLS * C, C), bf16),
            pltpu.VMEM((COLS, 2, N, C), bf16),
            pltpu.VMEM((COLS, HEADS, 2 * WIDTH, N), bf16),
            pltpu.VMEM((COLS, HEADS, WIDTH + 16, N), bf16),
            pltpu.VMEM((COLS, C, N), bf16),
            pltpu.VMEM((2, NX, N // NX, TILE), f32),
            pltpu.VMEM((2, NX, N // NX, TILE), f32),
            pltpu.VMEM((COLS, C, TILE), bf16),
        ],
        out_shape=jax.ShapeDtypeStruct((HEADS, N, C), bf16),
        cost_estimate=cost(40),
        compiler_params=pltpu.CompilerParams(vmem_limit_bytes=60 * 2**20),
        name="attend",
    )(place, upper, recv, keep, extra, *parts, *pieces)


def at(x, z, y, head):
    return (((x % NX) * NZ + z % NZ) * NY + y % NY) * HEADS + head


def send(value, dx, dz, dy=0):
    pairs = [
        (at(x, z, y, head), at(x + dx, z + dz, y + dy, head ^ (2 * dy)))
        for x in range(NX) for z in range(NZ) for y in range(NY) for head in range(HEADS)
    ]
    return lax.ppermute(value, ("dap", "head"), pairs)


def gather_bias(rows, out):
    beside = send(rows, 0, 0, 1)
    up = jnp.concatenate([send(rows, 0, 1), send(rows, 0, 1, 1)], 1)
    down = jnp.concatenate([send(rows, 0, -1), send(rows, 0, -1, 1)], 1)
    near = jnp.concatenate([rows, beside, up, down], 1)
    got = []
    for step in range(2, 4):
        up, down = send(up, 0, 1), send(down, 0, -1)
        got += [up, down]
    last = [send(up[:1], 0, 1), send(down[1:], 0, -1)]
    out, *last = lax.optimization_barrier((out, *last))
    last = jnp.concatenate(last, 0)
    far = jnp.concatenate(got + [last], 1)
    own = []
    for group in (near, far):
        left, right = send(group, 1, 0), send(group, -1, 0)
        own += [group, right, send(left[:1], 1, 0), send(right[1:], -1, 0), left]
    swap = [(h, h ^ 1) for h in range(HEADS)]
    return own + [lax.ppermute(piece, "head", swap) for piece in own], out


def body(pair, residue_mask, chain_breaks, w_query, w_key, w_value, w_gate, w_bias, w_out):
    dap = lax.axis_index("dap").astype(jnp.int32)
    head = lax.axis_index("head").astype(jnp.int32)
    place = jnp.stack([dap // (NZ * NY), (dap // NY) & (NZ - 1), dap & (NY - 1)])
    w_own = w_bias.T
    w_other = lax.ppermute(w_own, "head", [(h, h ^ 2) for h in range(HEADS)])
    upper = head >= 2
    w_two = jnp.concatenate(
        [jnp.where(upper, w_other, w_own), jnp.where(upper, w_own, w_other), jnp.zeros((14, C), bf16)], 0
    )
    mine = pack_call(w_query.T, w_key.T, w_value.T, w_gate.T, w_out)
    parts = [mine] + [lax.ppermute(mine, "head", [(h, h ^ n) for h in range(HEADS)]) for n in (2, 1, 3)]
    wide = lambda v: jnp.broadcast_to(v[None], (8, N))
    extra, keep = mask_call(place, wide(residue_mask), wide(chain_breaks))
    which, extra, keep = lax.optimization_barrier((head[None], extra, keep))
    normed, out = norm_call(pair, which)
    pieces, out = gather_bias(bias_call(normed, w_two), jnp.transpose(out, (2, 0, 1, 3)))
    recv = lax.all_to_all(out, "dap", 0, 0, tiled=True)
    update = attend_call(place, (head >> 1)[None], recv, keep, extra, parts, pieces)
    update = update.reshape(HEADS * DAP, ROWS, C)
    update = lax.all_to_all(update, ("head", "dap"), 0, 0, tiled=True)
    update = update.reshape(HEADS * DAP, ROWS, COLS, WIDTH)
    return jnp.transpose(update, (1, 2, 0, 3)).reshape(ROWS, N, WIDTH)


def solution(mesh):
    placed = (
        P("dap", None, None), P(), P(),
        P(None, "head"), P(None, "head"), P(None, "head"), P(None, "head"), P(None, "head"),
        P("head", None),
    )
    return jax.shard_map(
        body, mesh=mesh, in_specs=placed, out_specs=P("dap", None, "head"), check_vma=False
    )
```

```python
import functools
import math

import jax
import jax.numpy as jnp
from jax import lax
from jax.experimental import pallas as pl
from jax.experimental.pallas import tpu as pltpu
from jax.sharding import PartitionSpec as P

bf16 = jnp.bfloat16
f32 = jnp.float32

N = 1024
C = 128
HEADS = 4
WIDTH = 32
NX, NZ, NY = 4, 8, 2
DAP = NX * NZ * NY
ROWS = N // DAP
COLS = N // (DAP * HEADS)
TILE = 512
LOG2E = math.log2(math.e)
PENALTY = -2.0
MASKED = -1e9
NT = (((1,), (1,)), ((), ()))
TN = (((0,), (0,)), ((), ()))


def dot(a, b, dims=(((1,), (0,)), ((), ()))):
    return lax.dot_general(a, b, dims, preferred_element_type=f32)


def norm_kernel(head_ref, pair_ref, normed_ref, send_ref):
    average = jnp.full((C, C), 1.0 / C, bf16)
    twice = jnp.full((2 * C, C), 1.0 / C, bf16)
    for r in range(pair_ref.shape[0]):
        x = pair_ref[r]
        centered = x.astype(f32) - dot(x, average)
        square = centered * centered
        high = square.astype(bf16)
        low = (square - high.astype(f32)).astype(bf16)
        variance = dot(jnp.concatenate([high, low], 1), twice)
        normed_ref[r] = (centered * lax.rsqrt(variance + 1e-05)).astype(bf16)
        for c in range(COLS):
            start = pl.multiple_of(c * HEADS * DAP + head_ref[0] * DAP, DAP)
            send_ref[c, r] = normed_ref[r, pl.ds(start, DAP), :]


def norm_call(pair, head):
    step = 4
    return pl.pallas_call(
        norm_kernel,
        grid_spec=pltpu.PrefetchScalarGridSpec(
            num_scalar_prefetch=1,
            grid=(ROWS // step,),
            in_specs=[pl.BlockSpec((step, N, C), lambda r, h: (r, 0, 0))],
            out_specs=[
                pl.BlockSpec((step, N, C), lambda r, h: (r, 0, 0)),
                pl.BlockSpec((COLS, step, DAP, C), lambda r, h: (0, r, 0, 0)),
            ],
        ),
        out_shape=[
            jax.ShapeDtypeStruct((ROWS, N, C), bf16),
            jax.ShapeDtypeStruct((COLS, ROWS, DAP, C), bf16),
        ],
        cost_estimate=cost(6, 9 * 2**20),
        compiler_params=pltpu.CompilerParams(vmem_limit_bytes=32 * 2**20),
        name="norm",
    )(head, pair)


def cost(us, moved=0):
    return pl.CostEstimate(flops=int(us * 1.1e9), bytes_accessed=moved, transcendentals=0)


def bias_kernel(normed_ref, w_ref, out_ref):
    rows = normed_ref.shape[0]
    for r in range(rows):
        b = dot(w_ref[...], normed_ref[r], NT)
        out_ref[0, pl.ds(r, 1), :] = b[0:1].astype(bf16)
        out_ref[1, pl.ds(r, 1), :] = b[1:2].astype(bf16)


def bias_call(normed, w_two):
    return pl.pallas_call(
        bias_kernel,
        in_specs=[pl.BlockSpec(memory_space=pltpu.VMEM)] * 2,
        out_specs=pl.BlockSpec(memory_space=pltpu.VMEM),
        out_shape=jax.ShapeDtypeStruct((2, ROWS, N), bf16),
        cost_estimate=cost(1.5),
        compiler_params=pltpu.CompilerParams(vmem_limit_bytes=32 * 2**20),
        name="bias",
    )(normed, w_two)


def pack_kernel(wq, wk, wv, wg, wo, out_ref):
    for n, ref in enumerate((wq, wk, wv, wg, wo)):
        out_ref[n] = ref[...]


def pack_call(*weights):
    return pl.pallas_call(
        pack_kernel,
        in_specs=[pl.BlockSpec(memory_space=pltpu.VMEM)] * 5,
        out_specs=pl.BlockSpec(memory_space=pltpu.VMEM),
        out_shape=jax.ShapeDtypeStruct((5, WIDTH, C), bf16),
        cost_estimate=cost(1),
        name="pack",
    )(*weights)


def mask_kernel(place_ref, mask_ref, breaks_ref, extra_ref, keep_ref):
    chunk = N // NX
    row = breaks_ref[0:1, :].astype(f32)
    ones = jnp.ones((C, N), f32)
    breaks = (ones * row).astype(bf16)
    mask = (ones * (mask_ref[0:1, :] > 0).astype(f32)).astype(bf16)
    before = (
        lax.broadcasted_iota(jnp.int32, (N, N), 0) <= lax.broadcasted_iota(jnp.int32, (N, N), 1)
    )
    chain_row = dot(breaks[:16], jnp.where(before, 1.0, 0.0).astype(bf16))[0:1]
    for s in range(NX):
        k = jnp.concatenate(
            [
                lax.broadcasted_iota(jnp.int32, (ROWS, N), 0) + dap_of(place_ref, s, n, t) * ROWS
                for n in range(NZ) for t in range(NY)
            ],
            0,
        )
        j = lax.broadcasted_iota(jnp.int32, (chunk, N), 1)
        chain = dot(jnp.where(j <= k, 1.0, 0.0).astype(bf16), breaks, NT)
        keep = dot(jnp.where(j == k, 1.0, 0.0).astype(bf16), mask, NT)
        keep_ref[s] = keep.astype(bf16)
        for t in range(N // C):
            at = slice(t * C, (t + 1) * C)
            value = jnp.where(chain == chain_row[:, at], 0.0, PENALTY)
            extra_ref[s, :, at] = jnp.where(keep > 0.5, value, MASKED).astype(bf16)


def mask_call(place, mask, breaks):
    return pl.pallas_call(
        mask_kernel,
        in_specs=[pl.BlockSpec(memory_space=pltpu.SMEM)] + [pl.BlockSpec(memory_space=pltpu.VMEM)] * 2,
        out_specs=[pl.BlockSpec(memory_space=pltpu.VMEM)] * 2,
        out_shape=[
            jax.ShapeDtypeStruct((NX, N // NX, N), bf16),
            jax.ShapeDtypeStruct((NX, N // NX, C), bf16),
        ],
        cost_estimate=cost(2),
        compiler_params=pltpu.CompilerParams(vmem_limit_bytes=32 * 2**20),
        name="mask",
    )(place, mask, breaks)


def order_weights(upper_ref, parts, w_ref, spread_ref):
    for h in range(HEADS):
        low, high = parts[h // 2 * 2], parts[h // 2 * 2 + 1]
        w_ref[h] = jnp.where(upper_ref[0] == h % 2, low[...], high[...])
    w_out = jnp.concatenate([w_ref[h, 4] for h in range(HEADS)], 0)
    a = lax.broadcasted_iota(jnp.int32, (C, C), 0)
    b = lax.broadcasted_iota(jnp.int32, (C, C), 1)
    for o in range(HEADS):
        for c in range(COLS):
            pick = (b // WIDTH == c) & (a == b - c * WIDTH + o * WIDTH)
            moved = dot(w_out, jnp.where(pick, 1.0, 0.0).astype(bf16))
            spread_ref[o, c * C : (c + 1) * C] = moved.astype(bf16)


AROUND = (0, -1, 1, -2, 2, -3, 3, 4)


def dap_of(place_ref, s, n, t):
    x, z, y = place_ref[0], place_ref[1], place_ref[2]
    return ((x + s) & (NX - 1)) * (NZ * NY) + ((z + NZ + AROUND[n]) & (NZ - 1)) * NY + (y ^ t)


def project(c, place_ref, recv_ref, keep_ref, w_ref, k_ref, q_ref, v_ref, g_ref):
    chunk = N // NX
    weight = lambda n: w_ref[:, n].reshape(C, C)
    whole = recv_ref[:, c].reshape(N, C)
    q = (dot(weight(0), whole, NT) * WIDTH ** (-0.5)).astype(bf16)
    q = q.astype(f32) * LOG2E
    high = q.astype(bf16)
    low = (q - high.astype(f32)).astype(bf16)
    for h in range(HEADS):
        rows = slice(h * WIDTH, (h + 1) * WIDTH)
        q_ref[c, h, 0:WIDTH] = high[rows]
        q_ref[c, h, WIDTH : 2 * WIDTH] = low[rows]
    g_ref[c] = jax.nn.sigmoid(dot(weight(3), whole, NT)).astype(bf16)
    ones = jnp.where(lax.broadcasted_iota(jnp.int32, (16, chunk), 0) == 0, 1.0, 0.0).astype(bf16)
    for s in range(NX):
        rows = jnp.concatenate(
            [recv_ref[dap_of(place_ref, s, n, t), c] for n in range(NZ) for t in range(NY)], 0
        )
        here = slice(s * chunk, (s + 1) * chunk)
        for p in range(2):
            first, second = w_ref[2 * p, 1], w_ref[2 * p + 1, 1]
            wk = jnp.concatenate([first, first, second, second], 0)
            k_ref[c, p, here] = dot(rows, wk, NT).astype(bf16) * keep_ref[s]
        v = dot(weight(2), rows, NT).astype(bf16)
        for h in range(HEADS):
            v_ref[c, h, 0:WIDTH, here] = v[h * WIDTH : (h + 1) * WIDTH]
            v_ref[c, h, WIDTH : WIDTH + 16, here] = ones


def attend_kernel(
    place_ref, upper_ref, recv_ref, keep_ref, extra_ref, *rest
):
    parts, bias_refs = rest[:4], rest[4:14]
    out_ref, w_ref, wout_ref, k_ref, q_ref, v_ref, g_ref, comb, s_scr, gated = rest[14:]
    lanes = pl.ds(pl.multiple_of(pl.program_id(0) * TILE, TILE), TILE)

    @pl.when(pl.program_id(0) == 0)
    def _():
        order_weights(upper_ref, parts, w_ref, wout_ref)

        def step(c, carry):
            project(c, place_ref, recv_ref, keep_ref, w_ref, k_ref, q_ref, v_ref, g_ref)
            return carry

        lax.fori_loop(0, COLS, step, 0)

    chunk = N // NX
    zeros = jnp.zeros((2 * WIDTH, TILE), bf16)

    def bias(h, s):
        parts = bias_refs[5 * (h // 2) : 5 * (h // 2) + 5]
        return [parts[2 + h % 2][0] if s == 2 else parts[s if s < 2 else 4][h % 2]]

    def score(h, c, s, q, top):
        k = k_ref[c, h // 2, s * chunk : (s + 1) * chunk]
        scores = dot(k, q) + comb[h % 2, s]
        s_scr[c % 2, s] = scores
        high = jnp.max(scores.reshape(chunk // 8, 8, TILE), 0)
        return high if top is None else jnp.maximum(top, high)

    def weigh(h, c, s, top, total):
        weights = jnp.exp2(s_scr[c % 2, s] - top).astype(bf16)
        part = dot(v_ref[c, h, :, s * chunk : (s + 1) * chunk], weights)
        return part if total is None else total + part

    def finish(h, c, total):
        attended = (total[0:WIDTH] / total[WIDTH : WIDTH + 1]).astype(bf16).astype(f32)
        rows = slice(h * WIDTH, (h + 1) * WIDTH)
        gated[c, rows] = (g_ref[c, rows, lanes].astype(f32) * attended).astype(bf16)

    steps = [(h, c) for h in range(HEADS) for c in range(COLS)]
    before = None
    for h, c in steps + [(None, None)]:
        if h is not None:
            if c == 0:
                for s in range(NX):
                    start = 0
                    for part in bias(h, s):
                        here = slice(start, start + part.shape[0])
                        extra = extra_ref[s, here].astype(f32)
                        value = jnp.where(extra > 0.5 * MASKED, part.astype(f32) + extra, MASKED)
                        comb[h % 2, s, here] = value * LOG2E
                        start += part.shape[0]
            q = q_ref[c, h, :, lanes]
            q = jnp.concatenate([q, zeros] if h % 2 == 0 else [zeros, q], 0)
        top = total = None
        for s in range(NX):
            if h is not None:
                top = score(h, c, s, q, top)
            if before is not None:
                total = weigh(before[0], before[1], s, before[2], total)
        if before is not None:
            finish(before[0], before[1], total)
        if h is not None:
            before = (h, c, jnp.max(top, 0, keepdims=True))
    joined = gated[...].reshape(COLS * C, TILE)
    for o in range(HEADS):
        out_ref[o] = dot(joined, wout_ref[o], TN).astype(bf16)


def attend_call(place, upper, recv, keep, extra, parts, pieces):
    whole = lambda shape: pl.BlockSpec(shape, lambda t: (0,) * len(shape))
    along = lambda shape: pl.BlockSpec(shape, lambda t: (0,) * (len(shape) - 1) + (t,))
    return pl.pallas_call(
        attend_kernel,
        grid=(N // TILE,),
        in_specs=[
            pl.BlockSpec(memory_space=pltpu.SMEM),
            pl.BlockSpec(memory_space=pltpu.SMEM),
            whole((DAP, COLS, ROWS, C)),
            whole((NX, N // NX, C)),
            along((NX, N // NX, TILE)),
        ]
        + [whole((5, WIDTH, C))] * 4
        + [along(piece.shape[:2] + (TILE,)) for piece in pieces],
        out_specs=pl.BlockSpec((HEADS, TILE, C), lambda t: (0, t, 0)),
        scratch_shapes=[
            pltpu.VMEM((HEADS, 5, WIDTH, C), bf16),
            pltpu.VMEM((HEADS, COLS * C, C), bf16),
            pltpu.VMEM((COLS, 2, N, C), bf16),
            pltpu.VMEM((COLS, HEADS, 2 * WIDTH, N), bf16),
            pltpu.VMEM((COLS, HEADS, WIDTH + 16, N), bf16),
            pltpu.VMEM((COLS, C, N), bf16),
            pltpu.VMEM((2, NX, N // NX, TILE), f32),
            pltpu.VMEM((2, NX, N // NX, TILE), f32),
            pltpu.VMEM((COLS, C, TILE), bf16),
        ],
        out_shape=jax.ShapeDtypeStruct((HEADS, N, C), bf16),
        cost_estimate=cost(40),
        compiler_params=pltpu.CompilerParams(vmem_limit_bytes=60 * 2**20),
        name="attend",
    )(place, upper, recv, keep, extra, *parts, *pieces)


def at(x, z, y, head):
    return (((x % NX) * NZ + z % NZ) * NY + y % NY) * HEADS + head


def send(value, dx, dz, dy=0):
    pairs = [
        (at(x, z, y, head), at(x + dx, z + dz, y + dy, head ^ (2 * dy)))
        for x in range(NX) for z in range(NZ) for y in range(NY) for head in range(HEADS)
    ]
    return lax.ppermute(value, ("dap", "head"), pairs)


def gather_bias(rows, out):
    beside = send(rows, 0, 0, 1)
    up = jnp.concatenate([send(rows, 0, 1), send(rows, 0, 1, 1)], 1)
    down = jnp.concatenate([send(rows, 0, -1), send(rows, 0, -1, 1)], 1)
    near = jnp.concatenate([rows, beside, up, down], 1)
    got = []
    for step in range(2, 4):
        up, down = send(up, 0, 1), send(down, 0, -1)
        got += [up, down]
    last = [send(up[:1], 0, 1), send(down[1:], 0, -1)]
    out, *last = lax.optimization_barrier((out, *last))
    last = jnp.concatenate(last, 0)
    plane = jnp.concatenate([near] + got + [last], 1)
    left, right = send(plane, 1, 0), send(plane, -1, 0)
    own = [plane, right, send(left[:1], 1, 0), send(right[1:], -1, 0), left]
    swap = [(h, h ^ 1) for h in range(HEADS)]
    return own + [lax.ppermute(piece, "head", swap) for piece in own], out


def body(pair, residue_mask, chain_breaks, w_query, w_key, w_value, w_gate, w_bias, w_out):
    dap = lax.axis_index("dap").astype(jnp.int32)
    head = lax.axis_index("head").astype(jnp.int32)
    place = jnp.stack([dap // (NZ * NY), (dap // NY) & (NZ - 1), dap & (NY - 1)])
    w_own = w_bias.T
    w_other = lax.ppermute(w_own, "head", [(h, h ^ 2) for h in range(HEADS)])
    upper = head >= 2
    w_two = jnp.concatenate(
        [jnp.where(upper, w_other, w_own), jnp.where(upper, w_own, w_other), jnp.zeros((14, C), bf16)], 0
    )
    mine = pack_call(w_query.T, w_key.T, w_value.T, w_gate.T, w_out)
    parts = [mine] + [lax.ppermute(mine, "head", [(h, h ^ n) for h in range(HEADS)]) for n in (2, 1, 3)]
    wide = lambda v: v.reshape(1, N)
    extra, keep = mask_call(place, wide(residue_mask), wide(chain_breaks))
    which, extra, keep = lax.optimization_barrier((head[None], extra, keep))
    normed, out = norm_call(pair, which)
    pieces, out = gather_bias(bias_call(normed, w_two), jnp.transpose(out, (2, 0, 1, 3)))
    recv = lax.all_to_all(out, "dap", 0, 0, tiled=True)
    update = attend_call(place, (head >> 1)[None], recv, keep, extra, parts, pieces)
    update = update.reshape(HEADS * DAP, ROWS, C)
    update = lax.all_to_all(update, ("head", "dap"), 0, 0, tiled=True)
    update = update.reshape(HEADS * DAP, ROWS, COLS, WIDTH)
    return jnp.transpose(update, (1, 2, 0, 3)).reshape(ROWS, N, WIDTH)


def solution(mesh):
    placed = (
        P("dap", None, None), P(), P(),
        P(None, "head"), P(None, "head"), P(None, "head"), P(None, "head"), P(None, "head"),
        P("head", None),
    )
    return jax.shard_map(
        body, mesh=mesh, in_specs=placed, out_specs=P("dap", None, "head"), check_vma=False
    )
```

```python
import functools
import math

import jax
import jax.numpy as jnp
from jax import lax
from jax.experimental import pallas as pl
from jax.experimental.pallas import tpu as pltpu
from jax.sharding import PartitionSpec as P

bf16 = jnp.bfloat16
f32 = jnp.float32

N = 1024
C = 128
HEADS = 4
WIDTH = 32
NX, NZ, NY = 4, 8, 2
DAP = NX * NZ * NY
ROWS = N // DAP
COLS = N // (DAP * HEADS)
TILE = 512
LOG2E = math.log2(math.e)
PENALTY = -2.0
MASKED = -1e9
NT = (((1,), (1,)), ((), ()))
TN = (((0,), (0,)), ((), ()))


def dot(a, b, dims=(((1,), (0,)), ((), ()))):
    return lax.dot_general(a, b, dims, preferred_element_type=f32)


def norm_kernel(head_ref, pair_ref, normed_ref, send_ref):
    average = jnp.full((C, C), 1.0 / C, bf16)
    twice = jnp.full((2 * C, C), 1.0 / C, bf16)
    for r in range(pair_ref.shape[0]):
        x = pair_ref[r]
        centered = x.astype(f32) - dot(x, average)
        square = centered * centered
        high = square.astype(bf16)
        low = (square - high.astype(f32)).astype(bf16)
        variance = dot(jnp.concatenate([high, low], 1), twice)
        normed_ref[r] = (centered * lax.rsqrt(variance + 1e-05)).astype(bf16)
        for c in range(COLS):
            start = pl.multiple_of(c * HEADS * DAP + head_ref[0] * DAP, DAP)
            send_ref[c, r] = normed_ref[r, pl.ds(start, DAP), :]


def norm_call(pair, head):
    step = 4
    return pl.pallas_call(
        norm_kernel,
        grid_spec=pltpu.PrefetchScalarGridSpec(
            num_scalar_prefetch=1,
            grid=(ROWS // step,),
            in_specs=[pl.BlockSpec((step, N, C), lambda r, h: (r, 0, 0))],
            out_specs=[
                pl.BlockSpec((step, N, C), lambda r, h: (r, 0, 0)),
                pl.BlockSpec((COLS, step, DAP, C), lambda r, h: (0, r, 0, 0)),
            ],
        ),
        out_shape=[
            jax.ShapeDtypeStruct((ROWS, N, C), bf16),
            jax.ShapeDtypeStruct((COLS, ROWS, DAP, C), bf16),
        ],
        cost_estimate=cost(6, 9 * 2**20),
        compiler_params=pltpu.CompilerParams(vmem_limit_bytes=32 * 2**20),
        name="norm",
    )(head, pair)


def cost(us, moved=0):
    return pl.CostEstimate(flops=int(us * 1.1e9), bytes_accessed=moved, transcendentals=0)


def bias_kernel(normed_ref, w_ref, out_ref):
    rows = normed_ref.shape[0]
    for r in range(rows):
        b = dot(w_ref[...], normed_ref[r], NT)
        out_ref[0, pl.ds(r, 1), :] = b[0:1].astype(bf16)
        out_ref[1, pl.ds(r, 1), :] = b[1:2].astype(bf16)


def bias_call(normed, w_two):
    return pl.pallas_call(
        bias_kernel,
        in_specs=[pl.BlockSpec(memory_space=pltpu.VMEM)] * 2,
        out_specs=pl.BlockSpec(memory_space=pltpu.VMEM),
        out_shape=jax.ShapeDtypeStruct((2, ROWS, N), bf16),
        cost_estimate=cost(1.5),
        compiler_params=pltpu.CompilerParams(vmem_limit_bytes=32 * 2**20),
        name="bias",
    )(normed, w_two)


def pack_kernel(wq, wk, wv, wg, wo, out_ref):
    for n, ref in enumerate((wq, wk, wv, wg, wo)):
        out_ref[n] = ref[...]


def pack_call(*weights):
    return pl.pallas_call(
        pack_kernel,
        in_specs=[pl.BlockSpec(memory_space=pltpu.VMEM)] * 5,
        out_specs=pl.BlockSpec(memory_space=pltpu.VMEM),
        out_shape=jax.ShapeDtypeStruct((5, WIDTH, C), bf16),
        cost_estimate=cost(1),
        name="pack",
    )(*weights)


def mask_kernel(place_ref, mask_ref, breaks_ref, extra_ref, keep_ref):
    chunk = N // NX
    row = breaks_ref[0:1, :].astype(f32)
    ones = jnp.ones((C, N), f32)
    breaks = (ones * row).astype(bf16)
    mask = (ones * (mask_ref[0:1, :] > 0).astype(f32)).astype(bf16)
    before = (
        lax.broadcasted_iota(jnp.int32, (N, N), 0) <= lax.broadcasted_iota(jnp.int32, (N, N), 1)
    )
    chain_row = dot(breaks[:16], jnp.where(before, 1.0, 0.0).astype(bf16))[0:1]
    for s in range(NX):
        k = jnp.concatenate(
            [
                lax.broadcasted_iota(jnp.int32, (ROWS, N), 0) + dap_of(place_ref, s, n, t) * ROWS
                for n in range(NZ) for t in range(NY)
            ],
            0,
        )
        j = lax.broadcasted_iota(jnp.int32, (chunk, N), 1)
        chain = dot(jnp.where(j <= k, 1.0, 0.0).astype(bf16), breaks, NT)
        keep = dot(jnp.where(j == k, 1.0, 0.0).astype(bf16), mask, NT)
        keep_ref[s] = keep.astype(bf16)
        for t in range(N // C):
            at = slice(t * C, (t + 1) * C)
            value = jnp.where(chain == chain_row[:, at], 0.0, PENALTY)
            extra_ref[s, :, at] = jnp.where(keep > 0.5, value, MASKED).astype(bf16)


def mask_call(place, mask, breaks):
    return pl.pallas_call(
        mask_kernel,
        in_specs=[pl.BlockSpec(memory_space=pltpu.SMEM)] + [pl.BlockSpec(memory_space=pltpu.VMEM)] * 2,
        out_specs=[pl.BlockSpec(memory_space=pltpu.VMEM)] * 2,
        out_shape=[
            jax.ShapeDtypeStruct((NX, N // NX, N), bf16),
            jax.ShapeDtypeStruct((NX, N // NX, C), bf16),
        ],
        cost_estimate=cost(2),
        compiler_params=pltpu.CompilerParams(vmem_limit_bytes=32 * 2**20),
        name="mask",
    )(place, mask, breaks)


def order_weights(upper_ref, parts, w_ref, spread_ref):
    for h in range(HEADS):
        low, high = parts[h // 2 * 2], parts[h // 2 * 2 + 1]
        w_ref[h] = jnp.where(upper_ref[0] == h % 2, low[...], high[...])
    w_out = jnp.concatenate([w_ref[h, 4] for h in range(HEADS)], 0)
    a = lax.broadcasted_iota(jnp.int32, (C, C), 0)
    b = lax.broadcasted_iota(jnp.int32, (C, C), 1)
    for o in range(HEADS):
        for c in range(COLS):
            pick = (b // WIDTH == c) & (a == b - c * WIDTH + o * WIDTH)
            moved = dot(w_out, jnp.where(pick, 1.0, 0.0).astype(bf16))
            spread_ref[o, c * C : (c + 1) * C] = moved.astype(bf16)


AROUND = (0, -1, 1, -2, 2, -3, 3, 4)


def dap_of(place_ref, s, n, t):
    x, z, y = place_ref[0], place_ref[1], place_ref[2]
    return ((x + s) & (NX - 1)) * (NZ * NY) + ((z + NZ + AROUND[n]) & (NZ - 1)) * NY + (y ^ t)


def project(c, place_ref, recv_ref, keep_ref, w_ref, k_ref, q_ref, v_ref, g_ref):
    chunk = N // NX
    weight = lambda n: w_ref[:, n].reshape(C, C)
    whole = recv_ref[:, c].reshape(N, C)
    q = (dot(weight(0), whole, NT) * WIDTH ** (-0.5)).astype(bf16)
    q = q.astype(f32) * LOG2E
    high = q.astype(bf16)
    low = (q - high.astype(f32)).astype(bf16)
    for h in range(HEADS):
        rows = slice(h * WIDTH, (h + 1) * WIDTH)
        q_ref[c, h, 0:WIDTH] = high[rows]
        q_ref[c, h, WIDTH : 2 * WIDTH] = low[rows]
    g_ref[c] = jax.nn.sigmoid(dot(weight(3), whole, NT)).astype(bf16)
    ones = jnp.where(lax.broadcasted_iota(jnp.int32, (16, chunk), 0) == 0, 1.0, 0.0).astype(bf16)
    for s in range(NX):
        rows = jnp.concatenate(
            [recv_ref[dap_of(place_ref, s, n, t), c] for n in range(NZ) for t in range(NY)], 0
        )
        here = slice(s * chunk, (s + 1) * chunk)
        for p in range(2):
            first, second = w_ref[2 * p, 1], w_ref[2 * p + 1, 1]
            wk = jnp.concatenate([first, first, second, second], 0)
            k_ref[c, p, here] = dot(rows, wk, NT).astype(bf16) * keep_ref[s]
        v = dot(weight(2), rows, NT).astype(bf16)
        for h in range(HEADS):
            v_ref[c, h, 0:WIDTH, here] = v[h * WIDTH : (h + 1) * WIDTH]
            v_ref[c, h, WIDTH : WIDTH + 16, here] = ones


def attend_kernel(
    place_ref, upper_ref, recv_ref, keep_ref, extra_ref, *rest
):
    parts, bias_refs = rest[:4], rest[4:14]
    out_ref, w_ref, wout_ref, k_ref, q_ref, v_ref, g_ref, comb, s_scr, gated = rest[14:]
    lanes = pl.ds(pl.multiple_of(pl.program_id(0) * TILE, TILE), TILE)

    @pl.when(pl.program_id(0) == 0)
    def _():
        order_weights(upper_ref, parts, w_ref, wout_ref)

        def step(c, carry):
            project(c, place_ref, recv_ref, keep_ref, w_ref, k_ref, q_ref, v_ref, g_ref)
            return carry

        lax.fori_loop(0, COLS, step, 0)

    chunk = N // NX
    zeros = jnp.zeros((2 * WIDTH, TILE), bf16)

    def bias(h, s):
        parts = bias_refs[5 * (h // 2) : 5 * (h // 2) + 5]
        return [parts[2 + h % 2][0] if s == 2 else parts[s if s < 2 else 4][h % 2]]

    def score(h, c, s, q, top):
        k = k_ref[c, h // 2, s * chunk : (s + 1) * chunk]
        scores = dot(k, q) + comb[h % 2, s]
        s_scr[c % 2, s] = scores
        high = jnp.max(scores.reshape(chunk // 8, 8, TILE), 0)
        return high if top is None else jnp.maximum(top, high)

    def weigh(h, c, s, top, total):
        weights = jnp.exp2(s_scr[c % 2, s] - top).astype(bf16)
        part = dot(v_ref[c, h, :, s * chunk : (s + 1) * chunk], weights)
        return part if total is None else total + part

    def finish(h, c, total):
        attended = (total[0:WIDTH] / total[WIDTH : WIDTH + 1]).astype(bf16).astype(f32)
        rows = slice(h * WIDTH, (h + 1) * WIDTH)
        gated[c, rows] = (g_ref[c, rows, lanes].astype(f32) * attended).astype(bf16)

    steps = [(h, c) for h in range(HEADS) for c in range(COLS)]
    before = None
    for h, c in steps + [(None, None)]:
        if h is not None:
            if c == 0:
                for s in range(NX):
                    start = 0
                    for part in bias(h, s):
                        here = slice(start, start + part.shape[0])
                        extra = extra_ref[s, here].astype(f32)
                        value = jnp.where(extra > 0.5 * MASKED, part.astype(f32) + extra, MASKED)
                        comb[h % 2, s, here] = value * LOG2E
                        start += part.shape[0]
            q = q_ref[c, h, :, lanes]
            q = jnp.concatenate([q, zeros] if h % 2 == 0 else [zeros, q], 0)
        top = total = None
        for s in range(NX):
            if h is not None:
                top = score(h, c, s, q, top)
            if before is not None:
                total = weigh(before[0], before[1], s, before[2], total)
        if before is not None:
            finish(before[0], before[1], total)
        if h is not None:
            before = (h, c, jnp.max(top, 0, keepdims=True))
    joined = gated[...].reshape(COLS * C, TILE)
    for o in range(HEADS):
        out_ref[o] = dot(joined, wout_ref[o], TN).astype(bf16)


def attend_call(place, upper, recv, keep, extra, parts, pieces):
    whole = lambda shape: pl.BlockSpec(shape, lambda t: (0,) * len(shape))
    along = lambda shape: pl.BlockSpec(shape, lambda t: (0,) * (len(shape) - 1) + (t,))
    return pl.pallas_call(
        attend_kernel,
        grid=(N // TILE,),
        in_specs=[
            pl.BlockSpec(memory_space=pltpu.SMEM),
            pl.BlockSpec(memory_space=pltpu.SMEM),
            whole((DAP, COLS, ROWS, C)),
            whole((NX, N // NX, C)),
            along((NX, N // NX, TILE)),
        ]
        + [whole((5, WIDTH, C))] * 4
        + [along(piece.shape[:2] + (TILE,)) for piece in pieces],
        out_specs=pl.BlockSpec((HEADS, TILE, C), lambda t: (0, t, 0)),
        scratch_shapes=[
            pltpu.VMEM((HEADS, 5, WIDTH, C), bf16),
            pltpu.VMEM((HEADS, COLS * C, C), bf16),
            pltpu.VMEM((COLS, 2, N, C), bf16),
            pltpu.VMEM((COLS, HEADS, 2 * WIDTH, N), bf16),
            pltpu.VMEM((COLS, HEADS, WIDTH + 16, N), bf16),
            pltpu.VMEM((COLS, C, N), bf16),
            pltpu.VMEM((2, NX, N // NX, TILE), f32),
            pltpu.VMEM((2, NX, N // NX, TILE), f32),
            pltpu.VMEM((COLS, C, TILE), bf16),
        ],
        out_shape=jax.ShapeDtypeStruct((HEADS, N, C), bf16),
        cost_estimate=cost(40),
        compiler_params=pltpu.CompilerParams(vmem_limit_bytes=60 * 2**20),
        name="attend",
    )(place, upper, recv, keep, extra, *parts, *pieces)


def at(x, z, y, head):
    return (((x % NX) * NZ + z % NZ) * NY + y % NY) * HEADS + head


def send(value, dx, dz, dy=0):
    pairs = [
        (at(x, z, y, head), at(x + dx, z + dz, y + dy, head ^ (2 * dy)))
        for x in range(NX) for z in range(NZ) for y in range(NY) for head in range(HEADS)
    ]
    return lax.ppermute(value, ("dap", "head"), pairs)


def gather_bias(rows, out):
    both = jnp.concatenate([rows, send(rows, 0, 0, 1)], 1)
    up, down = send(both, 0, 1), send(both, 0, -1)
    near = jnp.concatenate([both, up, down], 1)
    got = []
    for step in range(2, 4):
        up, down = send(up, 0, 1), send(down, 0, -1)
        got += [up, down]
    last = [send(up[:1], 0, 1), send(down[1:], 0, -1)]
    out, *last = lax.optimization_barrier((out, *last))
    last = jnp.concatenate(last, 0)
    plane = jnp.concatenate([near] + got + [last], 1)
    left, right = send(plane, 1, 0), send(plane, -1, 0)
    own = [plane, right, send(left[:1], 1, 0), send(right[1:], -1, 0), left]
    swap = [(h, h ^ 1) for h in range(HEADS)]
    return own + [lax.ppermute(piece, "head", swap) for piece in own], out


def body(pair, residue_mask, chain_breaks, w_query, w_key, w_value, w_gate, w_bias, w_out):
    dap = lax.axis_index("dap").astype(jnp.int32)
    head = lax.axis_index("head").astype(jnp.int32)
    place = jnp.stack([dap // (NZ * NY), (dap // NY) & (NZ - 1), dap & (NY - 1)])
    w_own = w_bias.T
    w_other = lax.ppermute(w_own, "head", [(h, h ^ 2) for h in range(HEADS)])
    upper = head >= 2
    w_two = jnp.concatenate(
        [jnp.where(upper, w_other, w_own), jnp.where(upper, w_own, w_other), jnp.zeros((14, C), bf16)], 0
    )
    mine = pack_call(w_query.T, w_key.T, w_value.T, w_gate.T, w_out)
    parts = [mine] + [lax.ppermute(mine, "head", [(h, h ^ n) for h in range(HEADS)]) for n in (2, 1, 3)]
    wide = lambda v: v.reshape(1, N)
    extra, keep = mask_call(place, wide(residue_mask), wide(chain_breaks))
    which, extra, keep = lax.optimization_barrier((head[None], extra, keep))
    normed, out = norm_call(pair, which)
    pieces, out = gather_bias(bias_call(normed, w_two), jnp.transpose(out, (2, 0, 1, 3)))
    recv = lax.all_to_all(out, "dap", 0, 0, tiled=True)
    update = attend_call(place, (head >> 1)[None], recv, keep, extra, parts, pieces)
    update = update.reshape(HEADS * DAP, ROWS, C)
    update = lax.all_to_all(update, ("head", "dap"), 0, 0, tiled=True)
    update = update.reshape(HEADS * DAP, ROWS, COLS, WIDTH)
    return jnp.transpose(update, (1, 2, 0, 3)).reshape(ROWS, N, WIDTH)


def solution(mesh):
    placed = (
        P("dap", None, None), P(), P(),
        P(None, "head"), P(None, "head"), P(None, "head"), P(None, "head"), P(None, "head"),
        P("head", None),
    )
    return jax.shard_map(
        body, mesh=mesh, in_specs=placed, out_specs=P("dap", None, "head"), check_vma=False
    )
```
